768 devices in a mesh: replica: 32 (over y, x), expert: 24 (over z, core).
Axes of the slice: x: 4, y: 8, z: 12, core: 2. Of those that a mesh axis runs over, the one named last changes fastest.
Arguments:
- tokens: bfloat16 [32, 3072, 1024], P('replica', 'expert'), may hold values from -6 to 6
- cotangent: bfloat16 [32, 3072, 1024], P('replica', 'expert'), may hold values from -6 to 6
- w_in: bfloat16 [24, 1024, 2048], P('expert'), may hold values from -0.1875 to 0.1875
- w_out: bfloat16 [24, 2048, 1024], P('expert'), may hold values from -0.125 to 0.125
- gate_values: float32 [32, 24, 192], P('replica', 'expert'), may hold values from 0.05 to 1
- expert_ids: int32 [32, 24, 192], P('replica', 'expert'), may hold values from 0 to 3071, as said below
- valid_counts: int32 [32, 24], P('replica', 'expert'), may hold values from 10 to 192
Outputs:
- mixed_rows: bfloat16 [32, 3072, 1024], P('replica', 'expert')
- token_grad: bfloat16 [32, 3072, 1024], P('replica', 'expert')
- grad_w_in: bfloat16 [24, 1024, 2048], P('expert', 'replica')
- grad_w_out: bfloat16 [24, 2048, 1024], P('expert', 'replica')
The draws below stay inside these ranges and needn't reach their ends.
Inputs may be any that keep to these rules, and one draw needn't show every extreme that they name: `expert_ids`: live entries of an expert's list are distinct and ascending; entries past the live count are 0. Among the live entries of one list, at most 10 lie in one device's block of 128 tokens, and some list has exactly 10 in some block.
All inputs are finite; a program needn't handle non-finite values.
Results may differ from the reference program's by a relative error of at most 0.02.
Values may be sent and summed in bfloat16 or wider, within the bound.
A program may use at most 64 MiB of HBM per device.

```python
import math
import jax
import jax.numpy as jnp
from jax import lax

D = 1024
FF = 2048
TOK_DEV = 128
MOST = 10
EXPERTS = 24
CAP = 192
TOKENS = 3072
N_REPLICA = 32
N_EXPERT = 24


def shared_lists(key):
    count_key, order_key = jax.random.split(jax.random.fold_in(key, 101))
    expert_index = jnp.arange(EXPERTS, dtype=jnp.int32)
    source_index = jnp.arange(N_EXPERT, dtype=jnp.int32)
    pair_take = jax.random.randint(count_key, (N_REPLICA, EXPERTS, N_EXPERT), 0, MOST + 1).astype(jnp.int32)
    forced = (source_index[None, :] == (expert_index % min(N_EXPERT, 4))[:, None]) | (expert_index[:, None] == 0)
    pair_take = jnp.where(forced[None], MOST, pair_take).astype(jnp.int32)
    pair_starts = jnp.cumsum(pair_take, axis=-1).astype(jnp.int32) - pair_take
    kept_take = jnp.clip(CAP - pair_starts, 0, pair_take).astype(jnp.int32)
    kept_ends = pair_starts + kept_take
    totals = jnp.sum(kept_take, axis=-1).astype(jnp.int32)
    order_keys = jax.random.split(order_key, N_REPLICA * EXPERTS * N_EXPERT)

    def choose(one_key):
        return jnp.sort(jax.random.permutation(one_key, TOK_DEV)[:MOST].astype(jnp.int32))
    offsets = jax.vmap(choose)(order_keys).reshape(N_REPLICA, EXPERTS, N_EXPERT * MOST)
    slot_index = jnp.arange(CAP, dtype=jnp.int32)
    source_of = jnp.minimum(jnp.sum((kept_ends[:, :, None, :] <= slot_index[:, None]).astype(jnp.int32), axis=-1), N_EXPERT - 1).astype(jnp.int32)
    start_of = jnp.take_along_axis(pair_starts, source_of, axis=-1)
    position = jnp.clip(slot_index - start_of, 0, MOST - 1)
    local_offset = jnp.take_along_axis(offsets, source_of * MOST + position, axis=-1)
    live_slot = slot_index < totals[..., None]
    token_ids = jnp.where(live_slot, source_of * TOK_DEV + local_offset, 0).astype(jnp.int32)
    return (token_ids, totals)


def draw_expert_ids(key, part):
    shared = shared_lists(key)
    return shared[0]


def draw_valid_counts(key, part):
    shared = shared_lists(key)
    return shared[1]


def levels(rng, dims, cuts, least, largest):
    def one(axis_at, shards_of):
        heights = jax.random.uniform(jax.random.fold_in(jax.random.fold_in(rng, 6), axis_at), (shards_of,), jnp.float32, least / len(cuts), largest / len(cuts))
        return jnp.repeat(jnp.exp(heights), dims[axis_at] // shards_of).reshape((-1,) + (1,) * (len(dims) - axis_at - 1))

    factor_of = one(*cuts[0])
    for cut in cuts[1:]:
        factor_of = factor_of * one(*cut)
    return factor_of


def bell_draw(stream_key, dims, scale, limit, cuts=(), kind=jnp.bfloat16):
    drawn = jax.random.normal(stream_key, dims, jnp.float32) * scale
    if len(cuts) > 0:
        drawn = levels(stream_key, dims, cuts, -0.22, 0.18) * drawn
    return jnp.clip(drawn, min=-limit, max=limit).astype(kind)


def setup_inputs(seed: int = 0) -> dict:
    arg_keys = jax.random.split(jax.random.key(seed), 8)
    tokens = bell_draw(arg_keys[0], (N_REPLICA, TOKENS, D), 1.0, 6.0, ((0, 32), (1, 24)))
    cotangent = bell_draw(arg_keys[1], (N_REPLICA, TOKENS, D), 1.0, 6.0, ((0, 32), (1, 24)))
    w_in = bell_draw(arg_keys[2], (EXPERTS, D, FF), D ** -0.5, 0.1875, ((0, 24),))
    w_out = bell_draw(arg_keys[3], (EXPERTS, FF, D), FF ** -0.5, 0.125, ((0, 24),))
    gate_values = jnp.clip(jnp.exp(math.log(1.0) - 2.9957323 * jax.random.uniform(arg_keys[4], (N_REPLICA, EXPERTS, CAP), jnp.float32) ** levels(arg_keys[4], (N_REPLICA, EXPERTS, CAP), ((0, 32), (1, 24)), -0.2, 0.2)), 0.05, 1.0)
    expert_ids = draw_expert_ids(jax.random.fold_in(arg_keys[7], 71), 0)
    valid_counts = draw_valid_counts(jax.random.fold_in(arg_keys[7], 71), 0)
    return {"tokens": tokens, "cotangent": cotangent, "w_in": w_in, "w_out": w_out, "gate_values": gate_values, "expert_ids": expert_ids, "valid_counts": valid_counts}


def gelu_value(values):
    return 0.5 * values * (1.0 + jax.scipy.special.erf(values * 0.7071067811865476))


def gelu_slope(values):
    return 0.5 * (1.0 + jax.scipy.special.erf(values * 0.7071067811865476)) + values * jnp.exp(-0.5 * values * values) * 0.3989422804014327


def reference(tokens, cotangent, w_in, w_out, gate_values, expert_ids, valid_counts):
    wide_in = w_in.astype(jnp.float32)
    wide_out = w_out.astype(jnp.float32)
    slot_index = jnp.arange(CAP, dtype=jnp.int32)
    zero_bf = jnp.zeros((), jnp.bfloat16)

    def replica_pass(carried, inputs):
        acc_in, acc_out = carried
        batch_tokens, batch_cot, gate_rows, id_rows, count_rows = inputs
        valid_mask = (slot_index[None, :] < count_rows[:, None])[:, :, None]
        picked = jnp.where(valid_mask, batch_tokens[id_rows], zero_bf)
        picked_cot = jnp.where(valid_mask, batch_cot[id_rows], zero_bf)
        before = jnp.einsum("ecd,edf->ecf", picked.astype(jnp.float32), wide_in)
        hidden = gelu_value(before).astype(jnp.bfloat16)
        projected = jnp.einsum("ecf,efd->ecd", hidden.astype(jnp.float32), wide_out)
        weighted = (gate_rows[:, :, None] * projected).astype(jnp.bfloat16)
        upstream = (gate_rows[:, :, None] * picked_cot.astype(jnp.float32)).astype(jnp.bfloat16)
        hidden_grad = jnp.einsum("ecd,efd->ecf", upstream.astype(jnp.float32), wide_out)
        before_grad = (hidden_grad * gelu_slope(before)).astype(jnp.bfloat16)
        input_grad = jnp.einsum("ecf,edf->ecd", before_grad.astype(jnp.float32), wide_in).astype(jnp.bfloat16)
        term_in = jnp.einsum("ecd,ecf->edf", picked.astype(jnp.float32), before_grad.astype(jnp.float32))
        term_out = jnp.einsum("ecf,ecd->efd", hidden.astype(jnp.float32), upstream.astype(jnp.float32))
        flat_ids = id_rows.reshape(-1)
        mixed_rows = jnp.zeros((TOKENS, D), jnp.float32).at[flat_ids].add(weighted.reshape(-1, D).astype(jnp.float32)).astype(jnp.bfloat16)
        token_grad = jnp.zeros((TOKENS, D), jnp.float32).at[flat_ids].add(input_grad.reshape(-1, D).astype(jnp.float32)).astype(jnp.bfloat16)
        acc_in = acc_in + lax.optimization_barrier(term_in.astype(jnp.bfloat16)).astype(jnp.float32)
        acc_out = acc_out + lax.optimization_barrier(term_out.astype(jnp.bfloat16)).astype(jnp.float32)
        return (acc_in, acc_out), (mixed_rows, token_grad)

    start_state = (jnp.zeros((EXPERTS, D, FF), jnp.float32), jnp.zeros((EXPERTS, FF, D), jnp.float32))
    (acc_in, acc_out), (mixed_rows, token_grad) = lax.scan(replica_pass, start_state, (tokens, cotangent, gate_values, expert_ids, valid_counts))
    grad_w_in = (acc_in / N_REPLICA).astype(jnp.bfloat16)
    grad_w_out = (acc_out / N_REPLICA).astype(jnp.bfloat16)
    return mixed_rows, token_grad, grad_w_in, grad_w_out
```

```python
import jax
import jax.numpy as jnp
from jax import lax
from jax.experimental import pallas as pl
from jax.experimental.pallas import tpu as pltpu
from jax.sharding import PartitionSpec as P

D = 1024
FF = 2048
TOK = 128
CAP = 192
NE = 24
NY = 8
NX = 4
MOST = 10
PACK = 640
ROWS = NE * MOST
PAD = 256
BLK = FF // NY
BF = jnp.bfloat16
F32 = jnp.float32
I32 = jnp.int32
MESH = pl.DeviceIdType.MESH

ORDER = (4, 3, -3, 2, -2, 1, -1, 0)
IDX = {o: i for i, o in enumerate(ORDER)}
IDX[-4] = 0
SIGN = (1, -1)


def nn(a, b):
    return jnp.dot(a, b, preferred_element_type=F32)


def nt(a, b):
    return lax.dot_general(a, b, (((1,), (1,)), ((), ())), preferred_element_type=F32)


def tn(a, b):
    return lax.dot_general(a, b, (((0,), (0,)), ((), ())), preferred_element_type=F32)


def iota(shape, dim):
    return lax.broadcasted_iota(I32, shape, dim)


def div10(v):
    return (v * 6554) >> 16


def div5(v):
    return (v * 13108) >> 16


class Ring:
    def __init__(self, n, own, buf, ssem, rsem, peers, way):
        self.h = n // 2
        self.own, self.buf, self.ssem, self.rsem = own, buf, ssem, rsem
        self.peers, self.way = peers, way
        self.sent = []

    def copy(self, d, s, sub, src):
        return pltpu.make_async_remote_copy(
            src_ref=src,
            dst_ref=self.buf(d, s, sub),
            send_sem=self.ssem(d, s, sub),
            recv_sem=self.rsem(d, s, sub),
            device_id=self.peers[d],
            device_id_type=MESH,
        )

    def arrives(self, d, s, sub):
        return s >= 1 or self.way(sub) == d

    def send(self, d, s, sub):
        mine = self.own(SIGN[d] * (self.h - s), sub)
        src = mine
        if s >= 1 and self.arrives(d, s - 1, sub):
            src = self.buf(d, s - 1, sub)
            self.copy(d, s - 1, sub, src).wait_recv()
            src[...] = src[...] + mine[...]
        out = self.copy(d, s, sub, src)
        out.start()
        self.sent.append(out)

    def last(self, sub):
        total = self.own(0, sub)[...].astype(F32)
        for d in (0, 1):
            if self.arrives(d, self.h - 1, sub):
                got = self.buf(d, self.h - 1, sub)
                self.copy(d, self.h - 1, sub, got).wait_recv()
                total = total + got[...].astype(F32)
        return total

    def drain(self):
        for out in self.sent:
            out.wait_send()


def kernel(
    ids_c, ids_r, count, gate_r, tok_hbm, cot_hbm, w_in_hbm, w_out_hbm,
    mixed, tgrad, gwin, gwout,
    tok, cot, wi, wo, code_s, code_r, out_s, out_r, back_s, back_r, at,
    xs, us, proj, ig, ti, to, z1, z2,
    yr, xr, y2r, x2r,
    lsem, csem, asem, bsem, ys, yv, xsd, xv, y2s, y2v, x2s, x2v,
):
    rep = lax.axis_index("replica")
    me = lax.axis_index("expert")
    py = rep // NX
    px = rep % NX
    y_peers = [{"replica": ((py + g) % NY) * NX + px} for g in (1, NY - 1)]
    x_peers = [{"replica": py * NX + (px + g) % NX} for g in (1, NX - 1)]

    loads = [
        pltpu.make_async_copy(tok_hbm, tok, lsem.at[0]),
        pltpu.make_async_copy(cot_hbm, cot, lsem.at[1]),
    ]
    for i, o in enumerate(ORDER):
        b = (py + (o + NY)) % NY
        at_b = pl.ds(pl.multiple_of(b * BLK, BLK), BLK)
        loads.append(pltpu.make_async_copy(w_in_hbm.at[:, at_b], wi.at[i], lsem.at[2 + i]))
        loads.append(pltpu.make_async_copy(w_out_hbm.at[at_b, :], wo.at[i], lsem.at[10 + i]))
    for load in loads:
        load.start()

    barrier = pltpu.get_barrier_semaphore()

    @pl.loop(1, NE)
    def _(k):
        pl.semaphore_signal(
            barrier, inc=1, device_id={"expert": (me + k) % NE}, device_id_type=MESH
        )

    for peer in y_peers + x_peers:
        pl.semaphore_signal(barrier, inc=1, device_id=peer, device_id_type=MESH)

    n_live = count[...]
    live_c = iota((CAP, 1), 0) < n_live
    live_r = iota((1, CAP), 1) < n_live
    block_c = jnp.where(live_c, ids_c[...] >> 7, NE)
    block_r = ids_r[...] >> 7
    in_block = (block_c == iota((CAP, NE), 1)).astype(F32).astype(BF)
    in_place = ((ids_c[...] & (TOK - 1)) == iota((CAP, TOK), 1)).astype(F32).astype(BF)
    present = tn(in_block, in_place)
    before_me = (iota((TOK, TOK), 0) < iota((TOK, TOK), 1)).astype(F32).astype(BF)
    code = present * (nn(present.astype(BF), before_me) + 1.0)
    code_s[...] = jnp.broadcast_to(code[:, None, :], (NE, 16, TOK)).astype(BF)
    starts = jnp.sum((block_c < block_r).astype(I32), axis=0, keepdims=True)
    spot = MOST * block_r + iota((1, CAP), 1) - starts
    hit = (iota((PAD, CAP), 0) == spot) & live_r
    gate = jnp.sum(jnp.where(hit, gate_r[...], 0.0), axis=1, keepdims=True)

    pl.semaphore_wait(barrier, NE - 1 + 4)

    def scatter(src, dst, ssem, rsem):
        dst[pl.ds(me, 1)] = src[pl.ds(me, 1)]

        @pl.loop(0, NE - 1)
        def _(i):
            k = NE // 2 + ((i + 1) // 2) * (2 * (i % 2) - 1)
            to_e = (me + k) % NE
            pltpu.make_async_remote_copy(
                src_ref=src.at[to_e],
                dst_ref=dst.at[me],
                send_sem=ssem,
                recv_sem=rsem,
                device_id={"expert": to_e},
                device_id_type=MESH,
            ).start()

    def whole(ref, sem):
        part = ref.at[pl.ds(0, NE - 1)]
        pltpu.make_async_copy(part, part, sem).wait()

    scatter(code_s, code_r, csem.at[0], csem.at[1])
    loads[0].wait()
    loads[1].wait()
    whole(code_r, csem.at[1])

    row = iota((NE * 16, TOK), 0) & 15
    kind = jnp.where(row < MOST, 0, 1 + ((row - MOST) >> 1))
    coded = code_r[...].reshape(NE * 16, TOK).astype(F32)

    def chosen(q):
        wanted = jnp.where(row < MOST, row, ((row - MOST) & 1) * 5 + q) + 1
        return (coded == wanted.astype(F32)).astype(F32)

    def by_kind(v, kinds):
        out = v[:, : 128]
        for k in (1, 2, 3):
            out = jnp.where(kinds == k, v[:, k * 128 : (k + 1) * 128], out)
        return out

    for a, rows in enumerate((tok, cot)):
        for q in range(5):
            ahead = jnp.concatenate(
                [rows[:, q * 128 : (q + 1) * 128], rows[:, PACK:]], axis=1
            )
            picked = by_kind(nn(chosen(q).astype(BF), ahead), kind).astype(BF)
            out_s[a, :, :, q * 128 : (q + 1) * 128] = picked.reshape(NE, 16, 128)
        scatter(out_s.at[a], out_r.at[a], asem.at[0, a], asem.at[1, a])

    for q in range(5):
        one = chosen(q)
        for k in range(4):
            at[q, k * 128 : (k + 1) * 128, :] = jnp.where(kind == k, one, 0.0).T.astype(BF)

    gr = iota((80, 128), 0)
    gc = iota((80, 128), 1)
    g_src = div10(gr)
    g_j = gr - MOST * g_src
    g_five = div5(g_j)
    g_q = g_j - 5 * g_five
    same = (gc >> 4) == g_src
    spread = jnp.concatenate(
        [(same & ((gc & 15) == g_j)).astype(F32)]
        + [(same & ((gc & 15) == MOST + 2 * k + g_five)).astype(F32) for k in range(3)],
        axis=0,
    ).astype(BF)

    def unpack(a, put):
        for g in range(3):
            block = out_r[a, g * 8 : (g + 1) * 8].reshape(128, PACK)
            z = nn(spread, block)
            put(g, 0, z[:80])
            for k in range(3):
                zk = z[80 * (k + 1) : 80 * (k + 2)]
                v = zk[:, :128]
                for q in range(1, 5):
                    v = jnp.where(g_q == q, zk[:, q * 128 : (q + 1) * 128], v)
                put(g, PACK + k * 128, v)

    xs[ROWS:] = jnp.zeros((PAD - ROWS, D), BF)
    us[ROWS:] = jnp.zeros((PAD - ROWS, D), BF)

    def put_x(g, c, v):
        xs[g * 80 : (g + 1) * 80, c : c + v.shape[1]] = v.astype(BF)

    def put_u(g, c, v):
        us[g * 80 : (g + 1) * 80, c : c + v.shape[1]] = (
            gate[g * 80 : (g + 1) * 80] * v
        ).astype(BF)

    whole(out_r.at[0], asem.at[1, 0])
    unpack(0, put_x)
    whole(out_r.at[1], asem.at[1, 1])
    unpack(1, put_u)

    half_y = (pl.ds(0, NY // 2), pl.ds(NY // 2, NY // 2))
    flow_y = Ring(
        NY,
        lambda o, c: to.at[IDX[o], c],
        lambda d, s, c: yr.at[d, s, c],
        lambda d, s, c: ys.at[d, s, c],
        lambda d, s, c: yv.at[d, s, c],
        y_peers,
        lambda c: c // 2,
    )
    flow_x = Ring(
        NX,
        lambda o, sub: ti.at[sub[0], (px + (o + NX)) % NX, half_y[sub[1]]],
        lambda d, s, sub: xr.at[d, s, sub[0], sub[1]],
        lambda d, s, sub: xsd.at[d, s, sub[0], sub[1]],
        lambda d, s, sub: xv.at[d, s, sub[0], sub[1]],
        x_peers,
        lambda sub: sub[1],
    )
    flow_y2 = Ring(
        NY,
        lambda o, p: z1.at[(py + (o + NY)) % NY, half_y[p]],
        lambda d, s, p: y2r.at[d, s, p],
        lambda d, s, p: y2s.at[d, s, p],
        lambda d, s, p: y2v.at[d, s, p],
        y_peers,
        lambda p: p,
    )
    flow_x2 = Ring(
        NX,
        lambda o, p: z2.at[(px + (o + NX)) % NX, p],
        lambda d, s, p: x2r.at[d, s, p],
        lambda d, s, p: x2s.at[d, s, p],
        lambda d, s, p: x2v.at[d, s, p],
        x_peers,
        lambda p: p,
    )

    x_all = xs[...]
    u_all = us[...]
    for i, o in enumerate(ORDER):
        loads[2 + 2 * i].wait()
        loads[3 + 2 * i].wait()
        before = nn(x_all, wi[i])
        bell = 0.5 * (1.0 + lax.erf(before * 0.7071067811865476))
        hidden = (before * bell).astype(BF)
        slope = bell + before * jnp.exp(-0.5 * before * before) * 0.3989422804014327
        to[i] = tn(hidden, u_all).astype(BF).reshape(NX, 64, D)
        if o == 4:
            for c in range(NX):
                flow_y.send(c // 2, 0, c)
        if o == 3:
            for c in (2, 3):
                flow_y.send(0, 1, c)
        if o == -3:
            for c in (0, 1):
                flow_y.send(1, 1, c)
        grad = (nt(u_all, wo[i]) * slope).astype(BF)
        term = tn(x_all, grad).astype(BF).reshape(NY, NX, 32, BLK)
        for x in range(NX):
            ti[i, x] = term[:, x]
        for d in (0, 1):
            flow_x.send(d, 0, (i, d))
        for d in (0, 1):
            flow_x.send(d, 1, (i, 1 - d))
        if i == 0:
            proj[...] = nn(hidden, wo[i])
            ig[...] = nt(grad, wi[i])
        else:
            proj[...] += nn(hidden, wo[i])
            ig[...] += nt(grad, wi[i])
        if i == 4:
            for c in (0, 1):
                flow_y.send(0, 1, c)
                flow_y.send(1, 1, c + 2)

    hr = iota((128, 80), 0)
    hc = iota((128, 80), 1)
    h_row = hr & 15
    h_src = div10(hc)
    h_j = hc - MOST * h_src
    h_same = (hr >> 4) == h_src
    h_kind = kind[:128]
    for a, rows in enumerate((proj, ig)):
        for g in range(3):
            part = rows[g * 80 : (g + 1) * 80]
            if a == 0:
                part = gate[g * 80 : (g + 1) * 80] * part
            part = part.astype(BF)
            for q in range(5):
                wanted = jnp.where(h_row < MOST, h_row, ((h_row - MOST) & 1) * 5 + q)
                fold = (h_same & (h_j == wanted)).astype(F32).astype(BF)
                ahead = jnp.concatenate(
                    [part[:, q * 128 : (q + 1) * 128], part[:, PACK:]], axis=1
                )
                back_s[a, g * 8 : (g + 1) * 8, :, q * 128 : (q + 1) * 128] = (
                    by_kind(nn(fold, ahead), h_kind).astype(BF).reshape(8, 16, 128)
                )
        scatter(back_s.at[a], back_r.at[a], bsem.at[0, a], bsem.at[1, a])

    ways = [(d, c) for c in (2, 3, 0, 1) for d in (0, 1)]
    ways = [(d, c if d == 0 else (c + 2) % 4) for d, c in ways]
    for i in range(NY):
        d, c = ways[i]
        flow_y.send(d, 2, c)
        flow_x.send(0, 1, (i, 0))
        flow_x.send(1, 1, (i, 1))
    for i, o in enumerate(ORDER):
        d, c = ways[i]
        flow_y.send(d, 3, c)
        b = (py + (o + NY)) % NY
        for p in (0, 1):
            z1[half_y[p], pl.ds(b, 1)] = flow_x.last((i, p)).astype(BF)[:, None]
    for d in (0, 1):
        flow_y2.send(d, 0, d)
    for d in (0, 1):
        flow_y2.send(d, 1, 1 - d)
    for c in range(NX):
        z2[c] = flow_y.last(c).astype(BF).reshape(2, 32, D)
    for d in (0, 1):
        flow_x2.send(d, 0, d)
    for d in (0, 1):
        flow_x2.send(d, 1, 1 - d)
    for d in (0, 1):
        flow_y2.send(d, 1, d)
    for d in (0, 1):
        flow_x2.send(d, 1, d)
    for p in (0, 1):
        for d in (0, 1):
            flow_y2.send(d, 2, (1 - d + p) % 2)

    for a, dest in enumerate((mixed, tgrad)):
        whole(back_r.at[a], bsem.at[1, a])
        tail = [jnp.zeros((TOK, 128), F32) for _ in range(3)]
        for q in range(5):
            z = nn(at[q], back_r[a, :, :, q * 128 : (q + 1) * 128].reshape(NE * 16, 128))
            dest[:, q * 128 : (q + 1) * 128] = z[:128].astype(BF)
            for k in range(3):
                tail[k] = tail[k] + z[(k + 1) * 128 : (k + 2) * 128]
        for k in range(3):
            dest[:, PACK + k * 128 : PACK + (k + 1) * 128] = tail[k].astype(BF)

    for p in (0, 1):
        for d in (0, 1):
            flow_y2.send(d, 3, (1 - d + p) % 2)
    scale = 1.0 / (NX * NY)
    for p in (0, 1):
        gwout[p * 32 : (p + 1) * 32] = (flow_x2.last(p) * scale).astype(BF)
    for p in (0, 1):
        total = (flow_y2.last(p) * scale).astype(BF)
        for b in range(NY // 2):
            at_b = (p * (NY // 2) + b) * BLK
            gwin[:, at_b : at_b + BLK] = total[b]

    for flow in (flow_y, flow_x, flow_y2, flow_x2):
        flow.drain()
    whole(code_s, csem.at[0])
    for a in (0, 1):
        whole(out_s.at[a], asem.at[0, a])
        whole(back_s.at[a], bsem.at[0, a])


def per_device(tokens, cotangent, w_in, w_out, gate_values, expert_ids, valid_counts):
    vm = pl.BlockSpec(memory_space=pltpu.VMEM)
    hbm = pl.BlockSpec(memory_space=pl.ANY)
    dma = pltpu.SemaphoreType.DMA
    blocks = (2, NE, 16, PACK)
    mixed, tgrad, gwin, gwout = pl.pallas_call(
        kernel,
        out_shape=(
            jax.ShapeDtypeStruct((TOK, D), BF),
            jax.ShapeDtypeStruct((TOK, D), BF),
            jax.ShapeDtypeStruct((32, FF), BF),
            jax.ShapeDtypeStruct((64, D), BF),
        ),
        in_specs=[vm] * 4 + [hbm] * 4,
        out_specs=(vm,) * 4,
        scratch_shapes=[
            pltpu.VMEM((TOK, D), BF),
            pltpu.VMEM((TOK, D), BF),
            pltpu.VMEM((NY, D, BLK), BF),
            pltpu.VMEM((NY, BLK, D), BF),
            pltpu.VMEM((NE, 16, TOK), BF),
            pltpu.VMEM((NE, 16, TOK), BF),
            pltpu.VMEM(blocks, BF),
            pltpu.VMEM(blocks, BF),
            pltpu.VMEM(blocks, BF),
            pltpu.VMEM(blocks, BF),
            pltpu.VMEM((5, 512, NE * 16), BF),
            pltpu.VMEM((PAD, D), BF),
            pltpu.VMEM((PAD, D), BF),
            pltpu.VMEM((PAD, D), F32),
            pltpu.VMEM((PAD, D), F32),
            pltpu.VMEM((NY, NX, NY, 32, BLK), BF),
            pltpu.VMEM((NY, NX, 64, D), BF),
            pltpu.VMEM((NY, NY, 32, BLK), BF),
            pltpu.VMEM((NX, 2, 32, D), BF),
            pltpu.VMEM((2, 4, NX, 64, D), BF),
            pltpu.VMEM((2, 2, NY, 2, NY // 2, 32, BLK), BF),
            pltpu.VMEM((2, 4, 2, NY // 2, 32, BLK), BF),
            pltpu.VMEM((2, 2, 2, 32, D), BF),
            dma((18,)),
            dma((2,)),
            dma((2, 2)),
            dma((2, 2)),
            dma((2, 4, NX)),
            dma((2, 4, NX)),
            dma((2, 2, NY, 2)),
            dma((2, 2, NY, 2)),
            dma((2, 4, 2)),
            dma((2, 4, 2)),
            dma((2, 2, 2)),
            dma((2, 2, 2)),
        ],
        compiler_params=pltpu.CompilerParams(
            collective_id=0, has_side_effects=True, vmem_limit_bytes=56 * 1024 * 1024
        ),
        cost_estimate=pl.CostEstimate(
            flops=12 * PAD * D * FF, bytes_accessed=10 * 1024 * 1024, transcendentals=2 * PAD * FF
        ),
    )(
        expert_ids.reshape(CAP, 1),
        expert_ids.reshape(1, CAP),
        valid_counts,
        gate_values.reshape(1, CAP),
        tokens[0],
        cotangent[0],
        w_in[0],
        w_out[0],
    )
    return mixed[None], tgrad[None], gwin[None], gwout[None]


def solution(mesh):
    placed = (
        P("replica", "expert", None),
        P("replica", "expert", None),
        P("expert", None, None),
        P("expert", None, None),
        P("replica", "expert", None),
        P("replica", "expert", None),
        P("replica", "expert"),
    )
    return jax.shard_map(
        per_device,
        mesh=mesh,
        in_specs=placed,
        out_specs=(
            P("replica", "expert", None),
            P("replica", "expert", None),
            P("expert", "replica", None),
            P("expert", "replica", None),
        ),
        check_vma=False,
    )
```

```python
import jax
import jax.numpy as jnp
from jax import lax
from jax.experimental import pallas as pl
from jax.experimental.pallas import tpu as pltpu
from jax.sharding import PartitionSpec as P

D = 1024
FF = 2048
TOK = 128
CAP = 192
NE = 24
NY = 8
NX = 4
MOST = 10
NQ = 5
NC = D // 128
COLS = tuple(tuple(range(16 * q // MOST, (16 * q + 15) // MOST + 1)) for q in range(NQ))
EARLY = 384
E_TILES = 2
ROWS = NE * MOST
PAD = 256
BLK = FF // NY
BF = jnp.bfloat16
F32 = jnp.float32
I32 = jnp.int32
MESH = pl.DeviceIdType.MESH

ORDER = (4, 3, -3, 2, -2, 1, -1, 0)
IDX = {o: i for i, o in enumerate(ORDER)}
IDX[-4] = 0
SIGN = (1, -1)


def nn(a, b):
    return jnp.dot(a, b, preferred_element_type=F32)


def nt(a, b):
    return lax.dot_general(a, b, (((1,), (1,)), ((), ())), preferred_element_type=F32)


def tn(a, b):
    return lax.dot_general(a, b, (((0,), (0,)), ((), ())), preferred_element_type=F32)


def iota(shape, dim):
    return lax.broadcasted_iota(I32, shape, dim)


def div10(v):
    return (v * 6554) >> 16


PLAN = (
    ("toe", 0), ("e", 0, 0, 0), ("e", 1, 0, 1), ("proj",), ("toe", 1), ("toe", 2), ("e", 0, 1, 1),
    ("e", 1, 1, 0), ("toe", 3), ("toe", 4), ("toe", 5), ("toe", 6), ("e", 0, 1, 0), ("e", 1, 1, 1),
    ("toe", 7), ("e", 0, 2, 1), ("e", 1, 2, 0), ("e", 0, 2, 0), ("e", 1, 2, 1), ("cb",), ("ti", 0),
    ("x", 0, 0, (0, 0)), ("x", 1, 0, (0, 1)), ("x", 0, 1, (0, 1)), ("x", 1, 1, (0, 0)), ("tol", 0),
    ("y", 0, 0, 0), ("y", 0, 0, 1), ("y", 1, 0, 2), ("y", 1, 0, 3), ("ti", 1), ("x", 0, 0, (1, 0)),
    ("x", 1, 0, (1, 1)), ("x", 0, 1, (1, 1)), ("x", 1, 1, (1, 0)), ("ti", 2), ("x", 0, 0, (2, 0)),
    ("x", 1, 0, (2, 1)), ("x", 0, 1, (2, 1)), ("x", 1, 1, (2, 0)), ("x", 0, 1, (0, 0)),
    ("x", 1, 1, (0, 1)), ("tol", 1), ("y", 0, 1, 0), ("y", 0, 1, 2), ("y", 0, 1, 3), ("tol", 2),
    ("y", 1, 1, 2), ("y", 1, 1, 0), ("y", 1, 1, 1), ("ti", 3), ("y", 0, 1, 1), ("y", 1, 1, 3),
    ("x", 0, 0, (3, 0)), ("x", 1, 0, (3, 1)), ("x", 0, 1, (1, 0)), ("x", 1, 1, (1, 1)),
    ("x", 0, 1, (3, 1)), ("x", 1, 1, (3, 0)), ("ti", 4), ("x", 0, 0, (4, 0)), ("x", 1, 0, (4, 1)),
    ("tol", 3), ("y", 0, 2, 0), ("x", 0, 1, (2, 0)), ("x", 1, 1, (2, 1)), ("y", 0, 2, 2),
    ("tol", 4), ("y", 1, 2, 0), ("y", 1, 2, 2), ("x", 0, 1, (4, 1)), ("x", 1, 1, (4, 0)), ("ti", 5),
    ("z1", 0), ("y", 0, 2, 3), ("y", 1, 2, 1), ("x", 0, 0, (5, 0)), ("x", 1, 0, (5, 1)),
    ("x", 0, 1, (3, 0)), ("y", 0, 2, 1), ("x", 1, 1, (3, 1)), ("y", 1, 2, 3), ("x", 0, 1, (5, 1)),
    ("x", 1, 1, (5, 0)), ("z1", 1), ("y2", 0, 0, 0), ("tol", 5), ("y2", 1, 1, 0), ("tol", 6),
    ("ti", 6), ("x", 0, 0, (6, 0)), ("x", 1, 0, (6, 1)), ("x", 0, 1, (6, 1)), ("x", 1, 1, (6, 0)),
    ("e", 0, 3, 0), ("e", 1, 3, 0), ("x", 0, 1, (4, 0)), ("x", 1, 1, (4, 1)), ("e", 0, 3, 1),
    ("ti", 7), ("z1", 2), ("x", 0, 0, (7, 0)), ("x", 1, 0, (7, 1)), ("packg",), ("y2", 0, 1, 0),
    ("x", 0, 1, (5, 0)), ("x", 1, 1, (5, 1)), ("x", 0, 1, (7, 1)), ("x", 1, 1, (7, 0)),
    ("y2", 1, 2, 0), ("e", 1, 3, 1), ("z1", 3), ("y2", 1, 0, 1), ("y2", 0, 1, 1), ("y", 0, 3, 0),
    ("y", 0, 3, 1), ("y", 1, 3, 0), ("tol", 7), ("y", 1, 3, 1), ("y", 0, 3, 2), ("y2", 1, 3, 0),
    ("x", 0, 1, (6, 0)), ("x", 1, 1, (6, 1)), ("y2", 0, 2, 0), ("y2", 0, 2, 1), ("y", 1, 3, 2),
    ("y", 0, 3, 3), ("y", 1, 3, 3), ("mixed",), ("z1", 4), ("y2", 1, 1, 1), ("ze", 0), ("ze", 1),
    ("x", 0, 1, (7, 0)), ("x", 1, 1, (7, 1)), ("zl", 0), ("z1", 5), ("y2", 0, 0, 2),
    ("y2", 1, 1, 2), ("zl", 1), ("y2", 0, 3, 0), ("y2", 0, 3, 1), ("zl", 2), ("z1", 6), ("z1", 7),
    ("y2", 1, 0, 3), ("y2", 0, 1, 2), ("y2", 0, 1, 3), ("zl", 3), ("x2", 0, 0, 0), ("x2", 1, 0, 1),
    ("y2", 1, 2, 1), ("x2", 0, 1, 1), ("y2", 1, 2, 2), ("x2", 1, 1, 0), ("fi", 0), ("y2", 1, 1, 3),
    ("y2", 0, 2, 2), ("y2", 0, 2, 3), ("tgrad",), ("x2", 0, 1, 0), ("y2", 1, 2, 3), ("x2", 1, 1, 1),
    ("y2", 0, 3, 2), ("y2", 1, 3, 1), ("y2", 0, 3, 3), ("y2", 1, 3, 2), ("y2", 1, 3, 3), ("fo", 0),
    ("fi", 1), ("fo", 1), ("fi", 2), ("fi", 3),
)


class Ring:
    def __init__(self, n, own, buf, ssem, rsem, peers, way):
        self.h = n // 2
        self.own, self.buf, self.ssem, self.rsem = own, buf, ssem, rsem
        self.peers, self.way = peers, way
        self.sent = []

    def copy(self, d, s, sub, src):
        return pltpu.make_async_remote_copy(
            src_ref=src,
            dst_ref=self.buf(d, s, sub),
            send_sem=self.ssem(d, s, sub),
            recv_sem=self.rsem(d, s, sub),
            device_id=self.peers[d],
            device_id_type=MESH,
        )

    def arrives(self, d, s, sub):
        return s >= 1 or self.way(sub) == d

    def send(self, d, s, sub):
        mine = self.own(SIGN[d] * (self.h - s), sub)
        src = mine
        if s >= 1 and self.arrives(d, s - 1, sub):
            src = self.buf(d, s - 1, sub)
            self.copy(d, s - 1, sub, src).wait_recv()
            src[...] = src[...] + mine[...]
        out = self.copy(d, s, sub, src)
        out.start()
        self.sent.append(out)

    def last(self, sub):
        total = self.own(0, sub)[...].astype(F32)
        for d in (0, 1):
            if self.arrives(d, self.h - 1, sub):
                got = self.buf(d, self.h - 1, sub)
                self.copy(d, self.h - 1, sub, got).wait_recv()
                total = total + got[...].astype(F32)
        return total

    def drain(self):
        for out in self.sent:
            out.wait_send()


def kernel(
    ids_r, count, gate_r, tok_hbm, cot_hbm, w_in_hbm, w_out_hbm,
    mixed, tgrad, gwin, gwout,
    tok, cot, wi, wo, code_s, code_r, out_s, out_r, back_s, back_r, at,
    xs, xt, us, hid, hid_t, slopes, proj, ig, ti, toe, tol, z1, z2,
    yer, yr, xr, y2r, x2r,
    lsem, csem, asem, bsem, yes, yev, ys, yv, xsd, xv, y2s, y2v, x2s, x2v,
):
    rep = lax.axis_index("replica")
    me = lax.axis_index("expert")
    py = rep // NX
    px = rep % NX
    y_peers = [{"replica": ((py + g) % NY) * NX + px} for g in (1, NY - 1)]
    x_peers = [{"replica": py * NX + (px + g) % NX} for g in (1, NX - 1)]

    barrier = pltpu.get_barrier_semaphore()

    @pl.loop(1, NE)
    def _(k):
        pl.semaphore_signal(
            barrier, inc=1, device_id={"expert": (me + k) % NE}, device_id_type=MESH
        )

    for peer in y_peers + x_peers:
        pl.semaphore_signal(barrier, inc=1, device_id=peer, device_id_type=MESH)

    loads = [
        pltpu.make_async_copy(here, there, lsem.at[n])
        for n, (here, there) in enumerate(
            ((tok_hbm, tok), (cot_hbm, cot), (w_in_hbm, wi), (w_out_hbm, wo))
        )
    ]
    for load in loads:
        load.start()

    n_live = count[...]
    row_ids = ids_r[...]
    col_ids = jnp.broadcast_to(row_ids.astype(F32), (8, CAP)).T[:, :1].astype(I32)
    live_c = iota((CAP, 1), 0) < n_live
    live_r = iota((1, CAP), 1) < n_live
    block_c = jnp.where(live_c, col_ids >> 7, NE)
    block_r = row_ids >> 7
    in_block = (block_c == iota((CAP, NE), 1)).astype(F32).astype(BF)
    in_place = ((col_ids & (TOK - 1)) == iota((CAP, TOK), 1)).astype(F32).astype(BF)
    present = tn(in_block, in_place)
    before_me = (iota((TOK, TOK), 0) < iota((TOK, TOK), 1)).astype(F32).astype(BF)
    code = present * (nn(present.astype(BF), before_me) + 1.0)
    code_s[...] = jnp.broadcast_to(code[:, None, :], (NE, 16, TOK)).astype(BF)

    pl.semaphore_wait(barrier, NE - 1 + 4)

    def scatter(src, dst, ssem, rsem, part=None):
        def cut(ref, e):
            return ref.at[e] if part is None else ref.at[e, part]

        @pl.loop(0, NE - 1)
        def _(i):
            k = NE // 2 + ((i + 1) // 2) * (2 * (i % 2) - 1)
            to_e = (me + k) % NE
            pltpu.make_async_remote_copy(
                src_ref=cut(src, to_e),
                dst_ref=cut(dst, me),
                send_sem=ssem,
                recv_sem=rsem,
                device_id={"expert": to_e},
                device_id_type=MESH,
            ).start()

        if part is None:
            dst[pl.ds(me, 1)] = src[pl.ds(me, 1)]
        else:
            dst[pl.ds(me, 1), part] = src[pl.ds(me, 1), part]

    def whole(ref, sem, part=None):
        got = ref.at[pl.ds(0, NE - 1)] if part is None else ref.at[pl.ds(0, NE - 1), part]
        pltpu.make_async_copy(got, got, sem).wait()

    scatter(code_s, code_r, csem.at[0], csem.at[1])
    starts = jnp.sum((block_c < block_r).astype(I32), axis=0, keepdims=True)
    spot = MOST * block_r + iota((1, CAP), 1) - starts
    hit = (iota((PAD, CAP), 0) == spot) & live_r
    gate = jnp.sum(jnp.where(hit, gate_r[...], 0.0), axis=1, keepdims=True)
    loads[0].wait()
    loads[1].wait()
    whole(code_r, csem.at[1])

    row = iota((NE * 16, TOK), 0) & 15
    coded = code_r[...].reshape(NE * 16, TOK).astype(F32)

    def chosen(q):
        n = row + 16 * q
        return (coded == (n - MOST * div10(n) + 1).astype(F32)).astype(F32)

    def by_block(v, q, rows):
        block = div10(rows + 16 * q)
        out = v[:, :128]
        for k in range(1, len(COLS[q])):
            out = jnp.where(block == COLS[q][k], v[:, k * 128 : (k + 1) * 128], out)
        return out.astype(BF)

    def columns(q):
        return slice(COLS[q][0] * 128, (COLS[q][-1] + 1) * 128)

    def fill(a, rows):
        for q in range(NQ):
            v = nn(chosen(q).astype(BF), rows[:, columns(q)])
            out_s[a, :, q] = by_block(v, q, row).reshape(NE, 16, 128)

    first, second = pl.ds(0, E_TILES), pl.ds(E_TILES, NQ - E_TILES)
    fill(0, tok)
    scatter(out_s.at[0], out_r.at[0], asem.at[0, 0], asem.at[1, 0])
    fill(1, cot)
    scatter(out_s.at[1], out_r.at[1], asem.at[0, 1], asem.at[1, 1], first)

    for q in range(NQ):
        one = chosen(q)
        block = div10(row + 16 * q)
        for k, c in enumerate(COLS[q]):
            at[q, k * 128 : (k + 1) * 128, :] = jnp.where(block == c, one, 0.0).T.astype(BF)

    gr = iota((80, 128), 0)
    gc = iota((80, 128), 1)
    g_src = div10(gr)
    same = (gc >> 4) == g_src

    def unpack(a, blocks, put):
        for c in blocks:
            tiles = [q for q in range(NQ) if c in COLS[q]]
            spread = jnp.concatenate(
                [
                    (same & ((gc & 15) + 16 * q == MOST * c + gr - MOST * g_src)).astype(F32)
                    for q in tiles
                ],
                axis=1,
            ).astype(BF)
            came = jnp.concatenate(
                [
                    jnp.concatenate(
                        [out_r[a, g * 8 : (g + 1) * 8, q].reshape(128, 128) for g in range(3)],
                        axis=1,
                    )
                    for q in tiles
                ],
                axis=0,
            )
            v = nn(spread, came)
            for g in range(3):
                put(g, c, v[:, g * 128 : (g + 1) * 128])

    xs[ROWS:] = jnp.zeros((PAD - ROWS, D), BF)
    us[ROWS:] = jnp.zeros((PAD - ROWS, D), BF)

    def put_x(g, c, v):
        xs[g * 80 : (g + 1) * 80, c * 128 : (c + 1) * 128] = v.astype(BF)

    def put_u(g, c, v):
        us[g * 80 : (g + 1) * 80, c * 128 : (c + 1) * 128] = (
            gate[g * 80 : (g + 1) * 80] * v
        ).astype(BF)

    half = (pl.ds(0, NY // 2), pl.ds(NY // 2, NY // 2))
    flow_e = Ring(
        NY,
        lambda o, p: toe.at[IDX[o], pl.ds(2 * p, 2)],
        lambda d, s, p: yer.at[d, s, p],
        lambda d, s, p: yes.at[d, s, p],
        lambda d, s, p: yev.at[d, s, p],
        y_peers,
        lambda p: p,
    )
    flow_y = Ring(
        NY,
        lambda o, c: tol.at[IDX[o], c],
        lambda d, s, c: yr.at[d, s, c],
        lambda d, s, c: ys.at[d, s, c],
        lambda d, s, c: yv.at[d, s, c],
        y_peers,
        lambda c: c // 2,
    )
    flow_x = Ring(
        NX,
        lambda o, sub: ti.at[sub[0], (px + (o + NX)) % NX, half[sub[1]]],
        lambda d, s, sub: xr.at[d, s, sub[0], sub[1]],
        lambda d, s, sub: xsd.at[d, s, sub[0], sub[1]],
        lambda d, s, sub: xv.at[d, s, sub[0], sub[1]],
        x_peers,
        lambda sub: sub[1],
    )
    flow_y2 = Ring(
        NY,
        lambda o, p: z1.at[(py + (o + NY)) % NY, pl.ds(2 * p, 2)],
        lambda d, s, p: y2r.at[d, s, p],
        lambda d, s, p: y2s.at[d, s, p],
        lambda d, s, p: y2v.at[d, s, p],
        y_peers,
        lambda p: p % 2,
    )
    flow_x2 = Ring(
        NX,
        lambda o, p: z2.at[(px + (o + NX)) % NX, p],
        lambda d, s, p: x2r.at[d, s, p],
        lambda d, s, p: x2s.at[d, s, p],
        lambda d, s, p: x2v.at[d, s, p],
        x_peers,
        lambda p: p,
    )

    loads[2].wait()
    loads[3].wait()
    whole(out_r.at[0], asem.at[1, 0])
    scatter(out_s.at[1], out_r.at[1], asem.at[0, 2], asem.at[1, 2], second)
    unpack(0, range(NC), put_x)
    x_all = xs[...]
    for b in range(NY):
        before = nn(x_all, wi[:, b * BLK : (b + 1) * BLK])
        bell = 0.5 * (1.0 + lax.erf(before * 0.7071067811865476))
        hidden = (before * bell).astype(BF)
        hid[b] = hidden
        hid_t[b] = hidden.T
        slopes[b] = bell + before * jnp.exp(-0.5 * before * before) * 0.3989422804014327
    xt[...] = x_all.T

    hr = iota((128, 80), 0)
    hc = iota((128, 80), 1)
    h_src = div10(hc)
    h_same = (hr >> 4) == h_src

    def pack(a, rows):
        for q in range(NQ):
            n = (hr & 15) + 16 * q
            fold = (h_same & (hc - MOST * h_src == n - MOST * div10(n))).astype(F32).astype(BF)
            for g in range(3):
                v = nn(fold, rows(g)[:, columns(q)])
                back_s[a, g * 8 : (g + 1) * 8, q] = by_block(v, q, row[:128]).reshape(8, 16, 128)

    def term_out(i, u, dest):
        o = ORDER[i]
        term = nn(hid_t[(py + (o + NY)) % NY], u)
        dest[i] = term.astype(BF).reshape(NX, 64, u.shape[1])

    def term_in(i):
        grad = (nt(us[...], wo[i]) * slopes[i]).astype(BF)
        term = nn(xt[...], grad).astype(BF).reshape(NY, NX, 32, BLK)
        for x in range(NX):
            ti[i, x] = term[:, x]
        if i == 0:
            ig[...] = nt(grad, wi[:, i * BLK : (i + 1) * BLK])
        else:
            ig[...] += nt(grad, wi[:, i * BLK : (i + 1) * BLK])

    def project():
        for b in range(NY):
            if b == 0:
                proj[...] = nn(hid[b], wo[b])
            else:
                proj[...] += nn(hid[b], wo[b])
        pack(0, lambda g: (gate[g * 80 : (g + 1) * 80] * proj[g * 80 : (g + 1) * 80]).astype(BF))

    def second_cotangents():
        whole(out_r.at[1], asem.at[1, 2], second)
        scatter(back_s.at[0], back_r.at[0], bsem.at[0, 0], bsem.at[1, 0])
        unpack(1, range(EARLY // 128, NC), put_u)

    def input_grads_back():
        pack(1, lambda g: ig[g * 80 : (g + 1) * 80].astype(BF))
        scatter(back_s.at[1], back_r.at[1], bsem.at[0, 1], bsem.at[1, 1])

    def into_z1(i):
        for p in (0, 1):
            z1[half[p], i : i + 1] = flow_x.last((i, p)).astype(BF)[:, None]

    def early_z2(p):
        z2[2 * p : 2 * p + 2, :, :, :EARLY] = (
            flow_e.last(p).astype(BF).reshape(2, 2, 32, EARLY)
        )

    def late_z2(c):
        z2[c, :, :, EARLY:] = flow_y.last(c).astype(BF).reshape(2, 32, D - EARLY)

    def gather(a, dest):
        whole(back_r.at[a], bsem.at[1, a])
        sums = [None] * NC
        for q in range(NQ):
            z = nn(at[q, : len(COLS[q]) * 128], back_r[a, :, q].reshape(NE * 16, 128))
            for k, c in enumerate(COLS[q]):
                part = z[k * 128 : (k + 1) * 128]
                sums[c] = part if sums[c] is None else sums[c] + part
        for c in range(NC):
            dest[:, c * 128 : (c + 1) * 128] = sums[c].astype(BF)

    scale = 1.0 / (NX * NY)

    def finish_in(p):
        total = (flow_y2.last(p) * scale).astype(BF)
        for k in range(2):
            at_b = (2 * p + k) * BLK
            gwin[:, at_b : at_b + BLK] = total[k]

    def finish_out(p):
        gwout[p * 32 : (p + 1) * 32] = (flow_x2.last(p) * scale).astype(BF)

    steps = {
        "e": flow_e.send,
        "y": flow_y.send,
        "x": flow_x.send,
        "y2": flow_y2.send,
        "x2": flow_x2.send,
        "toe": lambda i: term_out(i, us[:, :EARLY], toe),
        "tol": lambda i: term_out(i, us[:, EARLY:], tol),
        "ti": term_in,
        "proj": project,
        "cb": second_cotangents,
        "packg": input_grads_back,
        "z1": into_z1,
        "ze": early_z2,
        "zl": late_z2,
        "mixed": lambda: gather(0, mixed),
        "tgrad": lambda: gather(1, tgrad),
        "fi": finish_in,
        "fo": finish_out,
    }
    whole(out_r.at[1], asem.at[1, 1], first)
    unpack(1, range(EARLY // 128), put_u)
    for name, *at_step in PLAN:
        steps[name](*at_step)

    for flow in (flow_e, flow_y, flow_x, flow_y2, flow_x2):
        flow.drain()
    whole(code_s, csem.at[0])
    whole(out_s.at[0], asem.at[0, 0])
    whole(out_s.at[1], asem.at[0, 1], first)
    whole(out_s.at[1], asem.at[0, 2], second)
    for a in (0, 1):
        whole(back_s.at[a], bsem.at[0, a])


def place(*refs):
    sems = refs[-1]
    made, out, held = refs[:4], refs[4:8], refs[8:12]
    for k in range(4):
        pltpu.make_async_copy(made[k], held[k], sems.at[0, k]).start()
    for k in range(4):
        pltpu.make_async_copy(made[k], held[k], sems.at[0, k]).wait()
        pltpu.make_async_copy(held[k], out[k], sems.at[1, k]).start()
    for k in range(4):
        pltpu.make_async_copy(held[k], out[k], sems.at[1, k]).wait()


def per_device(tokens, cotangent, w_in, w_out, gate_values, expert_ids, valid_counts):
    vm = pl.BlockSpec(memory_space=pltpu.VMEM)
    hbm = pl.BlockSpec(memory_space=pl.ANY)
    dma = pltpu.SemaphoreType.DMA
    blocks = (2, NE, NQ, 16, 128)
    results = (
        jax.ShapeDtypeStruct((TOK, D), BF),
        jax.ShapeDtypeStruct((TOK, D), BF),
        jax.ShapeDtypeStruct((32, FF), BF),
        jax.ShapeDtypeStruct((64, D), BF),
    )
    late = D - EARLY
    made = pl.pallas_call(
        kernel,
        out_shape=results,
        in_specs=[vm] * 3 + [hbm] * 4,
        out_specs=(vm,) * 4,
        scratch_shapes=[
            pltpu.VMEM((TOK, D), BF),
            pltpu.VMEM((TOK, D), BF),
            pltpu.VMEM((D, FF), BF),
            pltpu.VMEM((NY, BLK, D), BF),
            pltpu.VMEM((NE, 16, TOK), BF),
            pltpu.VMEM((NE, 16, TOK), BF),
            pltpu.VMEM(blocks, BF),
            pltpu.VMEM(blocks, BF),
            pltpu.VMEM(blocks, BF),
            pltpu.VMEM(blocks, BF),
            pltpu.VMEM((NQ, 384, NE * 16), BF),
            pltpu.VMEM((PAD, D), BF),
            pltpu.VMEM((D, PAD), BF),
            pltpu.VMEM((PAD, D), BF),
            pltpu.VMEM((NY, PAD, BLK), BF),
            pltpu.VMEM((NY, BLK, PAD), BF),
            pltpu.VMEM((NY, PAD, BLK), F32),
            pltpu.VMEM((PAD, D), F32),
            pltpu.VMEM((PAD, D), F32),
            pltpu.VMEM((NY, NX, NY, 32, BLK), BF),
            pltpu.VMEM((NY, NX, 64, EARLY), BF),
            pltpu.VMEM((NY, NX, 64, late), BF),
            pltpu.VMEM((NY, NY, 32, BLK), BF),
            pltpu.VMEM((NX, 2, 32, D), BF),
            pltpu.VMEM((2, 4, 2, 2, 64, EARLY), BF),
            pltpu.VMEM((2, 4, NX, 64, late), BF),
            pltpu.VMEM((2, 2, NY, 2, NY // 2, 32, BLK), BF),
            pltpu.VMEM((2, 4, 4, 2, 32, BLK), BF),
            pltpu.VMEM((2, 2, 2, 32, D), BF),
            dma((4,)),
            dma((2,)),
            dma((2, 3)),
            dma((2, 2)),
            dma((2, 4, 2)),
            dma((2, 4, 2)),
            dma((2, 4, NX)),
            dma((2, 4, NX)),
            dma((2, 2, NY, 2)),
            dma((2, 2, NY, 2)),
            dma((2, 4, 4)),
            dma((2, 4, 4)),
            dma((2, 2, 2)),
            dma((2, 2, 2)),
        ],
        compiler_params=pltpu.CompilerParams(
            collective_id=0, has_side_effects=True, vmem_limit_bytes=56 * 1024 * 1024
        ),
        cost_estimate=pl.CostEstimate(
            flops=12 * PAD * D * FF, bytes_accessed=10 * 1024 * 1024, transcendentals=2 * PAD * FF
        ),
    )(
        expert_ids.reshape(1, CAP),
        valid_counts,
        gate_values.reshape(1, CAP),
        tokens[0],
        cotangent[0],
        w_in[0],
        w_out.reshape(NY, BLK, D),
    )
    made = pl.pallas_call(
        place,
        out_shape=results,
        in_specs=[hbm] * 4,
        out_specs=(hbm,) * 4,
        scratch_shapes=[pltpu.VMEM(r.shape, r.dtype) for r in results] + [dma((2, 4))],
        compiler_params=pltpu.CompilerParams(vmem_limit_bytes=60 * 1024 * 1024),
    )(*made)
    return tuple(array[None] for array in made)


def solution(mesh):
    placed = (
        P("replica", "expert", None),
        P("replica", "expert", None),
        P("expert", None, None),
        P("expert", None, None),
        P("replica", "expert", None),
        P("replica", "expert", None),
        P("replica", "expert"),
    )
    return jax.shard_map(
        per_device,
        mesh=mesh,
        in_specs=placed,
        out_specs=(
            P("replica", "expert", None),
            P("replica", "expert", None),
            P("expert", "replica", None),
            P("expert", "replica", None),
        ),
        check_vma=False,
    )
```

```python
import jax
import jax.numpy as jnp
from jax import lax
from jax.experimental import pallas as pl
from jax.experimental.pallas import tpu as pltpu
from jax.sharding import PartitionSpec as P

D = 1024
FF = 2048
TOK = 128
CAP = 192
NE = 24
NY = 8
NX = 4
MOST = 10
NQ = 5
NC = D // 128
COLS = tuple(tuple(range(16 * q // MOST, (16 * q + 15) // MOST + 1)) for q in range(NQ))
EARLY = 384
E_TILES = 2
ROWS = NE * MOST
PAD = 256
BLK = FF // NY
BF = jnp.bfloat16
F32 = jnp.float32
I32 = jnp.int32
MESH = pl.DeviceIdType.MESH

ORDER = (4, 3, -3, 2, -2, 1, -1, 0)
AWAY = ORDER[:-1]
IDX = {o: i for i, o in enumerate(ORDER)}
IDX[-4] = 0
SIGN = (1, -1)


def nn(a, b):
    return jnp.dot(a, b, preferred_element_type=F32)


def nt(a, b):
    return lax.dot_general(a, b, (((1,), (1,)), ((), ())), preferred_element_type=F32)


def tn(a, b):
    return lax.dot_general(a, b, (((0,), (0,)), ((), ())), preferred_element_type=F32)


def iota(shape, dim):
    return lax.broadcasted_iota(I32, shape, dim)


def div10(v):
    return (v * 6554) >> 16


PLAN = (
    ("toe", 0), ("e", 0, 0, 0), ("e", 1, 0, 1), ("toe", 1), ("toe", 2), ("e", 0, 1, 1),
    ("e", 1, 1, 0), ("toe", 3), ("toe", 4), ("proj",), ("toe", 5), ("toe", 6), ("toe", 7),
    ("e", 0, 1, 0), ("e", 1, 1, 1), ("e", 0, 2, 1), ("e", 1, 2, 0), ("e", 0, 2, 0), ("e", 1, 2, 1),
    ("cb",), ("ti", 0), ("x", 0, 0, (0, 0)), ("x", 1, 0, (0, 1)), ("x", 0, 1, (0, 1)),
    ("x", 1, 1, (0, 0)), ("tol", 0), ("y", 0, 0, 0), ("y", 1, 0, 2), ("y", 0, 0, 1), ("y", 1, 0, 3),
    ("ti", 1), ("x", 0, 0, (1, 0)), ("x", 1, 0, (1, 1)), ("x", 0, 1, (1, 1)), ("x", 1, 1, (1, 0)),
    ("tol", 1), ("y", 0, 1, 2), ("ti", 2), ("x", 0, 0, (2, 0)), ("x", 1, 0, (2, 1)),
    ("x", 0, 1, (2, 1)), ("x", 1, 1, (2, 0)), ("y", 0, 1, 3), ("tol", 2), ("y", 1, 1, 0),
    ("x", 0, 1, (0, 0)), ("x", 1, 1, (0, 1)), ("y", 1, 1, 2), ("y", 0, 1, 0), ("y", 1, 1, 1),
    ("ti", 3), ("x", 0, 0, (3, 0)), ("x", 1, 0, (3, 1)), ("tol", 3), ("y", 0, 1, 1),
    ("x", 0, 1, (1, 0)), ("x", 1, 1, (1, 1)), ("y", 1, 1, 3), ("ti", 4), ("y", 0, 2, 2),
    ("x", 0, 0, (4, 0)), ("x", 1, 0, (4, 1)), ("e", 1, 3, 0), ("e", 0, 3, 0), ("e", 1, 3, 1),
    ("x", 0, 1, (2, 0)), ("x", 1, 1, (2, 1)), ("tol", 4), ("y", 0, 2, 3), ("x", 0, 1, (3, 1)),
    ("x", 1, 1, (3, 0)), ("y", 1, 2, 0), ("ti", 5), ("z1", 0), ("y", 0, 2, 0), ("x", 0, 0, (5, 0)),
    ("x", 1, 0, (5, 1)), ("y", 1, 2, 1), ("ti", 6), ("x", 0, 0, (6, 0)), ("x", 1, 0, (6, 1)),
    ("tol", 5), ("y", 0, 2, 1), ("y", 1, 2, 2), ("z1", 1), ("x", 0, 1, (3, 0)), ("x", 1, 1, (3, 1)),
    ("tol", 6), ("y", 0, 3, 2), ("y", 1, 2, 3), ("x", 0, 1, (4, 0)), ("x", 1, 1, (4, 1)), ("ti", 7),
    ("z1", 2), ("packg",), ("x", 0, 1, (5, 0)), ("x", 1, 1, (5, 1)), ("x", 0, 1, (4, 1)),
    ("x", 1, 1, (4, 0)), ("y", 0, 3, 0), ("x", 0, 1, (5, 1)), ("y", 1, 3, 0), ("x", 1, 1, (5, 0)),
    ("y", 0, 3, 3), ("y", 1, 3, 1), ("x", 0, 1, (6, 0)), ("x", 1, 1, (6, 1)), ("z1", 3),
    ("y", 0, 3, 1), ("y", 1, 3, 2), ("x", 0, 1, (6, 1)), ("x", 1, 1, (6, 0)), ("y2", 0, 0, 0),
    ("y2", 1, 0, 1), ("y", 1, 3, 3), ("y2", 0, 1, 1), ("e", 0, 3, 1), ("x", 0, 0, (7, 0)),
    ("x", 1, 0, (7, 1)), ("ze", 0), ("mixed",), ("x", 0, 1, (7, 1)), ("x", 1, 1, (7, 0)),
    ("y2", 1, 1, 0), ("tol", 7), ("z1", 4), ("zl", 0), ("z1", 5), ("y2", 0, 0, 2), ("y2", 1, 1, 2),
    ("zl", 1), ("zl", 2), ("y2", 0, 1, 0), ("y2", 1, 1, 1), ("y2", 0, 2, 1), ("z1", 6),
    ("y2", 1, 0, 3), ("y2", 0, 1, 3), ("zl", 3), ("x", 0, 1, (7, 0)), ("x", 1, 1, (7, 1)),
    ("y2", 1, 2, 0), ("y2", 0, 1, 2), ("y2", 1, 2, 2), ("ze", 1), ("x2", 0, 0, 0), ("x2", 1, 0, 1),
    ("y2", 1, 1, 3), ("y2", 0, 2, 0), ("y2", 1, 2, 1), ("y2", 0, 2, 3), ("x2", 0, 1, 1),
    ("x2", 1, 1, 0), ("y2", 0, 3, 1), ("y2", 1, 3, 0), ("y2", 0, 2, 2), ("z1", 7), ("dd", -3),
    ("dd", 3), ("dd", -2), ("y2", 1, 2, 3), ("dd", 2), ("dd", 4), ("dd", 1), ("x2", 0, 1, 0),
    ("x2", 1, 1, 1), ("tgrad",), ("dd", -1), ("y2", 0, 3, 0), ("y2", 1, 3, 1), ("y2", 0, 3, 2),
    ("y2", 1, 3, 2), ("y2", 0, 3, 3), ("y2", 1, 3, 3), ("fo", 0), ("fo", 1), ("fd",), ("fi", 0),
    ("fi", 1), ("fi", 2), ("fi", 3),
)


class Ring:
    def __init__(self, n, own, buf, ssem, rsem, peers, way):
        self.h = n // 2
        self.own, self.buf, self.ssem, self.rsem = own, buf, ssem, rsem
        self.peers, self.way = peers, way
        self.sent = []

    def copy(self, d, s, sub, src):
        return pltpu.make_async_remote_copy(
            src_ref=src,
            dst_ref=self.buf(d, s, sub),
            send_sem=self.ssem(d, s, sub),
            recv_sem=self.rsem(d, s, sub),
            device_id=self.peers[d],
            device_id_type=MESH,
        )

    def arrives(self, d, s, sub):
        return s >= 1 or self.way(sub) == d

    def send(self, d, s, sub):
        mine = self.own(SIGN[d] * (self.h - s), sub)
        src = mine
        if s >= 1 and self.arrives(d, s - 1, sub):
            src = self.buf(d, s - 1, sub)
            self.copy(d, s - 1, sub, src).wait_recv()
            src[...] = src[...] + mine[...]
        out = self.copy(d, s, sub, src)
        out.start()
        self.sent.append(out)

    def last(self, sub):
        total = self.own(0, sub)[...].astype(F32)
        for d in (0, 1):
            if self.arrives(d, self.h - 1, sub):
                got = self.buf(d, self.h - 1, sub)
                self.copy(d, self.h - 1, sub, got).wait_recv()
                total = total + got[...].astype(F32)
        return total

    def drain(self):
        for out in self.sent:
            out.wait_send()


class Spread:
    def __init__(self, own, buf, ssem, rsem, peer):
        self.own, self.buf, self.ssem, self.rsem, self.peer = own, buf, ssem, rsem, peer
        self.sent = []

    def copy(self, o, src):
        k = AWAY.index(o)
        return pltpu.make_async_remote_copy(
            src_ref=src,
            dst_ref=self.buf.at[k],
            send_sem=self.ssem.at[k],
            recv_sem=self.rsem.at[k],
            device_id=self.peer(o),
            device_id_type=MESH,
        )

    def send(self, o):
        out = self.copy(o, self.own(o))
        out.start()
        self.sent.append(out)

    def last(self):
        total = self.own(0)[...].astype(F32)
        for k, o in enumerate(AWAY):
            self.copy(o, self.buf.at[k]).wait_recv()
            total = total + self.buf[k].astype(F32)
        return total

    def drain(self):
        for out in self.sent:
            out.wait_send()


def kernel(
    ids_hbm, count_hbm, gate_hbm, tok_hbm, cot_hbm, w_in_hbm, w_out_hbm,
    mixed_hbm, tgrad_hbm, gwin_hbm, gwout_hbm,
    ids_r, count, gate_r, mixed, tgrad, gwin, gwout,
    tok, cot, wi, wo, code_s, code_r, out_s, out_r, back_s, back_r, at,
    xs, xt, us, hid, hid_t, slopes, proj, ig, ti, toe, tol, z1, z2,
    yer, yr, xr, y2r, x2r, ddr,
    lsem, osem, csem, asem, bsem, yes, yev, ys, yv, xsd, xv, y2s, y2v, x2s, x2v, dds, ddv,
):
    rep = lax.axis_index("replica")
    me = lax.axis_index("expert")
    py = rep // NX
    px = rep % NX
    y_peers = [{"replica": ((py + g) % NY) * NX + px} for g in (1, NY - 1)]
    x_peers = [{"replica": py * NX + (px + g) % NX} for g in (1, NX - 1)]

    barrier = pltpu.get_barrier_semaphore()

    @pl.loop(1, NE)
    def _(k):
        pl.semaphore_signal(
            barrier, inc=1, device_id={"expert": (me + k) % NE}, device_id_type=MESH
        )

    for g in range(1, NY):
        peer = {"replica": ((py + g) % NY) * NX + px}
        pl.semaphore_signal(barrier, inc=1, device_id=peer, device_id_type=MESH)
    for peer in x_peers:
        pl.semaphore_signal(barrier, inc=1, device_id=peer, device_id_type=MESH)

    loads = [
        pltpu.make_async_copy(here, there, lsem.at[n])
        for n, (here, there) in enumerate(
            (
                (tok_hbm, tok), (cot_hbm, cot), (w_in_hbm, wi), (w_out_hbm, wo),
                (ids_hbm, ids_r), (count_hbm, count), (gate_hbm, gate_r),
            )
        )
    ]
    loads = loads[4:] + loads[:4]
    for load in loads:
        load.start()
    for load in loads[:3]:
        load.wait()
    loads = loads[3:]

    n_live = count[...]
    row_ids = ids_r[...]
    col_ids = jnp.broadcast_to(row_ids.astype(F32), (8, CAP)).T[:, :1].astype(I32)
    live_c = iota((CAP, 1), 0) < n_live
    live_r = iota((1, CAP), 1) < n_live
    block_c = jnp.where(live_c, col_ids >> 7, NE)
    block_r = row_ids >> 7
    in_block = (block_c == iota((CAP, NE), 1)).astype(F32).astype(BF)
    in_place = ((col_ids & (TOK - 1)) == iota((CAP, TOK), 1)).astype(F32).astype(BF)
    present = tn(in_block, in_place)
    before_me = (iota((TOK, TOK), 0) < iota((TOK, TOK), 1)).astype(F32).astype(BF)
    code = present * (nn(present.astype(BF), before_me) + 1.0)
    code_s[...] = jnp.broadcast_to(code[:, None, :], (NE, 16, TOK)).astype(BF)

    pl.semaphore_wait(barrier, NE - 1 + NY - 1 + 2)

    def scatter(src, dst, ssem, rsem, part=None):
        def cut(ref, e):
            return ref.at[e] if part is None else ref.at[e, part]

        @pl.loop(0, NE - 1)
        def _(i):
            k = NE // 2 + ((i + 1) // 2) * (2 * (i % 2) - 1)
            to_e = (me + k) % NE
            pltpu.make_async_remote_copy(
                src_ref=cut(src, to_e),
                dst_ref=cut(dst, me),
                send_sem=ssem,
                recv_sem=rsem,
                device_id={"expert": to_e},
                device_id_type=MESH,
            ).start()

        if part is None:
            dst[pl.ds(me, 1)] = src[pl.ds(me, 1)]
        else:
            dst[pl.ds(me, 1), part] = src[pl.ds(me, 1), part]

    def whole(ref, sem, part=None):
        got = ref.at[pl.ds(0, NE - 1)] if part is None else ref.at[pl.ds(0, NE - 1), part]
        pltpu.make_async_copy(got, got, sem).wait()

    scatter(code_s, code_r, csem.at[0], csem.at[1])
    starts = jnp.sum((block_c < block_r).astype(I32), axis=0, keepdims=True)
    spot = MOST * block_r + iota((1, CAP), 1) - starts
    hit = (iota((PAD, CAP), 0) == spot) & live_r
    gate = jnp.sum(jnp.where(hit, gate_r[...], 0.0), axis=1, keepdims=True)
    loads[0].wait()
    loads[1].wait()
    whole(code_r, csem.at[1])

    row = iota((NE * 16, TOK), 0) & 15
    coded = code_r[...].reshape(NE * 16, TOK).astype(F32)

    def chosen(q):
        n = row + 16 * q
        return (coded == (n - MOST * div10(n) + 1).astype(F32)).astype(F32)

    def by_block(v, q, rows):
        block = div10(rows + 16 * q)
        out = v[:, :128]
        for k in range(1, len(COLS[q])):
            out = jnp.where(block == COLS[q][k], v[:, k * 128 : (k + 1) * 128], out)
        return out.astype(BF)

    def columns(q):
        return slice(COLS[q][0] * 128, (COLS[q][-1] + 1) * 128)

    def fill(a, rows):
        for q in range(NQ):
            v = nn(chosen(q).astype(BF), rows[:, columns(q)])
            out_s[a, :, q] = by_block(v, q, row).reshape(NE, 16, 128)

    first, second = pl.ds(0, E_TILES), pl.ds(E_TILES, NQ - E_TILES)
    fill(0, tok)
    scatter(out_s.at[0], out_r.at[0], asem.at[0, 0], asem.at[1, 0])
    fill(1, cot)
    scatter(out_s.at[1], out_r.at[1], asem.at[0, 1], asem.at[1, 1], first)

    for q in range(NQ):
        one = chosen(q)
        block = div10(row + 16 * q)
        for k, c in enumerate(COLS[q]):
            at[q, k * 128 : (k + 1) * 128, :] = jnp.where(block == c, one, 0.0).T.astype(BF)

    gr = iota((80, 128), 0)
    gc = iota((80, 128), 1)
    g_src = div10(gr)
    same = (gc >> 4) == g_src

    def unpack(a, blocks, put):
        for c in blocks:
            tiles = [q for q in range(NQ) if c in COLS[q]]
            spread = jnp.concatenate(
                [
                    (same & ((gc & 15) + 16 * q == MOST * c + gr - MOST * g_src)).astype(F32)
                    for q in tiles
                ],
                axis=1,
            ).astype(BF)
            came = jnp.concatenate(
                [
                    jnp.concatenate(
                        [out_r[a, g * 8 : (g + 1) * 8, q].reshape(128, 128) for g in range(3)],
                        axis=1,
                    )
                    for q in tiles
                ],
                axis=0,
            )
            v = nn(spread, came)
            for g in range(3):
                put(g, c, v[:, g * 128 : (g + 1) * 128])

    xs[ROWS:] = jnp.zeros((PAD - ROWS, D), BF)
    us[ROWS:] = jnp.zeros((PAD - ROWS, D), BF)

    def put_x(g, c, v):
        xs[g * 80 : (g + 1) * 80, c * 128 : (c + 1) * 128] = v.astype(BF)

    def put_u(g, c, v):
        us[g * 80 : (g + 1) * 80, c * 128 : (c + 1) * 128] = (
            gate[g * 80 : (g + 1) * 80] * v
        ).astype(BF)

    half = (pl.ds(0, NY // 2), pl.ds(NY // 2, NY // 2))
    flow_e = Ring(
        NY,
        lambda o, p: toe.at[IDX[o], pl.ds(2 * p, 2)],
        lambda d, s, p: yer.at[d, s, p],
        lambda d, s, p: yes.at[d, s, p],
        lambda d, s, p: yev.at[d, s, p],
        y_peers,
        lambda p: p,
    )
    flow_y = Ring(
        NY,
        lambda o, c: tol.at[IDX[o], c],
        lambda d, s, c: yr.at[d, s, c],
        lambda d, s, c: ys.at[d, s, c],
        lambda d, s, c: yv.at[d, s, c],
        y_peers,
        lambda c: c // 2,
    )
    flow_x = Ring(
        NX,
        lambda o, sub: ti.at[sub[0], (px + (o + NX)) % NX, half[sub[1]]],
        lambda d, s, sub: xr.at[d, s, sub[0], sub[1]],
        lambda d, s, sub: xsd.at[d, s, sub[0], sub[1]],
        lambda d, s, sub: xv.at[d, s, sub[0], sub[1]],
        x_peers,
        lambda sub: sub[1],
    )
    flow_y2 = Ring(
        NY,
        lambda o, p: z1.at[(py + (o + NY)) % NY, pl.ds(2 * p, 2 - p // 3)],
        lambda d, s, p: y2r.at[d, s, p, pl.ds(0, 2 - p // 3)],
        lambda d, s, p: y2s.at[d, s, p],
        lambda d, s, p: y2v.at[d, s, p],
        y_peers,
        lambda p: p % 2,
    )
    flow_d = Spread(
        lambda o: z1.at[(py + (o + NY)) % NY, NY - 1],
        ddr,
        dds,
        ddv,
        lambda o: {"replica": ((py + (o + NY)) % NY) * NX + px},
    )
    flow_x2 = Ring(
        NX,
        lambda o, p: z2.at[(px + (o + NX)) % NX, p],
        lambda d, s, p: x2r.at[d, s, p],
        lambda d, s, p: x2s.at[d, s, p],
        lambda d, s, p: x2v.at[d, s, p],
        x_peers,
        lambda p: p,
    )

    loads[2].wait()
    loads[3].wait()
    whole(out_r.at[0], asem.at[1, 0])
    scatter(out_s.at[1], out_r.at[1], asem.at[0, 2], asem.at[1, 2], second)
    unpack(0, range(NC), put_x)
    x_all = xs[...]
    for b in range(NY):
        before = nn(x_all, wi[:, b * BLK : (b + 1) * BLK])
        bell = 0.5 * (1.0 + lax.erf(before * 0.7071067811865476))
        hidden = (before * bell).astype(BF)
        hid[b] = hidden
        hid_t[b] = hidden.T
        slopes[b] = bell + before * jnp.exp(-0.5 * before * before) * 0.3989422804014327
    xt[...] = x_all.T

    hr = iota((128, 80), 0)
    hc = iota((128, 80), 1)
    h_src = div10(hc)
    h_same = (hr >> 4) == h_src

    def pack(a, rows):
        for q in range(NQ):
            n = (hr & 15) + 16 * q
            fold = (h_same & (hc - MOST * h_src == n - MOST * div10(n))).astype(F32).astype(BF)
            for g in range(3):
                v = nn(fold, rows(g)[:, columns(q)])
                back_s[a, g * 8 : (g + 1) * 8, q] = by_block(v, q, row[:128]).reshape(8, 16, 128)

    def term_out(i, u, dest):
        o = ORDER[i]
        term = nn(hid_t[(py + (o + NY)) % NY], u)
        dest[i] = term.astype(BF).reshape(NX, 64, u.shape[1])

    def term_in(i):
        grad = (nt(us[...], wo[i]) * slopes[i]).astype(BF)
        term = nn(xt[...], grad).astype(BF).reshape(NY, NX, 32, BLK)
        for x in range(NX):
            ti[i, x] = term[:, x]
        if i == 0:
            ig[...] = nt(grad, wi[:, i * BLK : (i + 1) * BLK])
        else:
            ig[...] += nt(grad, wi[:, i * BLK : (i + 1) * BLK])

    def project():
        for b in range(NY):
            if b == 0:
                proj[...] = nn(hid[b], wo[b])
            else:
                proj[...] += nn(hid[b], wo[b])
        pack(0, lambda g: (gate[g * 80 : (g + 1) * 80] * proj[g * 80 : (g + 1) * 80]).astype(BF))

    def second_cotangents():
        whole(out_r.at[1], asem.at[1, 2], second)
        scatter(back_s.at[0], back_r.at[0], bsem.at[0, 0], bsem.at[1, 0])
        unpack(1, range(EARLY // 128, NC), put_u)

    def input_grads_back():
        pack(1, lambda g: ig[g * 80 : (g + 1) * 80].astype(BF))
        scatter(back_s.at[1], back_r.at[1], bsem.at[0, 1], bsem.at[1, 1])

    def into_z1(i):
        for p in (0, 1):
            z1[half[p], i : i + 1] = flow_x.last((i, p)).astype(BF)[:, None]

    def early_z2(p):
        z2[2 * p : 2 * p + 2, :, :, :EARLY] = (
            flow_e.last(p).astype(BF).reshape(2, 2, 32, EARLY)
        )

    def late_z2(c):
        z2[c, :, :, EARLY:] = flow_y.last(c).astype(BF).reshape(2, 32, D - EARLY)

    stores = [
        pltpu.make_async_copy(here, there, osem.at[n])
        for n, (here, there) in enumerate(
            ((mixed, mixed_hbm), (tgrad, tgrad_hbm), (gwin, gwin_hbm), (gwout, gwout_hbm))
        )
    ]

    def gather(a, dest):
        whole(back_r.at[a], bsem.at[1, a])
        sums = [None] * NC
        for q in range(NQ):
            z = nn(at[q, : len(COLS[q]) * 128], back_r[a, :, q].reshape(NE * 16, 128))
            for k, c in enumerate(COLS[q]):
                part = z[k * 128 : (k + 1) * 128]
                sums[c] = part if sums[c] is None else sums[c] + part
        for c in range(NC):
            dest[:, c * 128 : (c + 1) * 128] = sums[c].astype(BF)
        stores[a].start()

    scale = 1.0 / (NX * NY)

    def finish_in(p):
        total = (flow_y2.last(p) * scale).astype(BF)
        for k in range(2 - p // 3):
            at_b = (2 * p + k) * BLK
            gwin[:, at_b : at_b + BLK] = total[k]

    def finish_direct():
        gwin[:, FF - BLK :] = (flow_d.last() * scale).astype(BF)

    def finish_out(p):
        gwout[p * 32 : (p + 1) * 32] = (flow_x2.last(p) * scale).astype(BF)

    steps = {
        "e": flow_e.send,
        "y": flow_y.send,
        "x": flow_x.send,
        "y2": flow_y2.send,
        "x2": flow_x2.send,
        "toe": lambda i: term_out(i, us[:, :EARLY], toe),
        "tol": lambda i: term_out(i, us[:, EARLY:], tol),
        "ti": term_in,
        "proj": project,
        "cb": second_cotangents,
        "packg": input_grads_back,
        "z1": into_z1,
        "ze": early_z2,
        "zl": late_z2,
        "mixed": lambda: gather(0, mixed),
        "tgrad": lambda: gather(1, tgrad),
        "fi": finish_in,
        "fo": finish_out,
        "dd": flow_d.send,
        "fd": finish_direct,
    }
    whole(out_r.at[1], asem.at[1, 1], first)
    unpack(1, range(EARLY // 128), put_u)
    for name, *at_step in PLAN:
        steps[name](*at_step)

    stores[2].start()
    stores[3].start()
    for flow in (flow_e, flow_y, flow_x, flow_y2, flow_x2, flow_d):
        flow.drain()
    whole(code_s, csem.at[0])
    whole(out_s.at[0], asem.at[0, 0])
    whole(out_s.at[1], asem.at[0, 1], first)
    whole(out_s.at[1], asem.at[0, 2], second)
    for a in (0, 1):
        whole(back_s.at[a], bsem.at[0, a])
    for store in stores:
        store.wait()


def place(*refs):
    sems = refs[-1]
    made, out, held = refs[:4], refs[4:8], refs[8:12]
    for k in range(4):
        pltpu.make_async_copy(made[k], held[k], sems.at[0, k]).start()
    for k in range(4):
        pltpu.make_async_copy(made[k], held[k], sems.at[0, k]).wait()
        pltpu.make_async_copy(held[k], out[k], sems.at[1, k]).start()
    for k in range(4):
        pltpu.make_async_copy(held[k], out[k], sems.at[1, k]).wait()


def per_device(tokens, cotangent, w_in, w_out, gate_values, expert_ids, valid_counts):
    hbm = pl.BlockSpec(memory_space=pl.ANY)
    dma = pltpu.SemaphoreType.DMA
    blocks = (2, NE, NQ, 16, 128)
    results = (
        jax.ShapeDtypeStruct((TOK, D), BF),
        jax.ShapeDtypeStruct((TOK, D), BF),
        jax.ShapeDtypeStruct((32, FF), BF),
        jax.ShapeDtypeStruct((64, D), BF),
    )
    late = D - EARLY
    made = pl.pallas_call(
        kernel,
        out_shape=results,
        in_specs=[hbm] * 7,
        out_specs=(hbm,) * 4,
        scratch_shapes=[
            pltpu.VMEM((1, CAP), I32),
            pltpu.VMEM((1, 1), I32),
            pltpu.VMEM((1, CAP), F32),
        ]
        + [pltpu.VMEM(r.shape, r.dtype) for r in results]
        + [
            pltpu.VMEM((TOK, D), BF),
            pltpu.VMEM((TOK, D), BF),
            pltpu.VMEM((D, FF), BF),
            pltpu.VMEM((NY, BLK, D), BF),
            pltpu.VMEM((NE, 16, TOK), BF),
            pltpu.VMEM((NE, 16, TOK), BF),
            pltpu.VMEM(blocks, BF),
            pltpu.VMEM(blocks, BF),
            pltpu.VMEM(blocks, BF),
            pltpu.VMEM(blocks, BF),
            pltpu.VMEM((NQ, 384, NE * 16), BF),
            pltpu.VMEM((PAD, D), BF),
            pltpu.VMEM((D, PAD), BF),
            pltpu.VMEM((PAD, D), BF),
            pltpu.VMEM((NY, PAD, BLK), BF),
            pltpu.VMEM((NY, BLK, PAD), BF),
            pltpu.VMEM((NY, PAD, BLK), F32),
            pltpu.VMEM((PAD, D), F32),
            pltpu.VMEM((PAD, D), F32),
            pltpu.VMEM((NY, NX, NY, 32, BLK), BF),
            pltpu.VMEM((NY, NX, 64, EARLY), BF),
            pltpu.VMEM((NY, NX, 64, late), BF),
            pltpu.VMEM((NY, NY, 32, BLK), BF),
            pltpu.VMEM((NX, 2, 32, D), BF),
            pltpu.VMEM((2, 4, 2, 2, 64, EARLY), BF),
            pltpu.VMEM((2, 4, NX, 64, late), BF),
            pltpu.VMEM((2, 2, NY, 2, NY // 2, 32, BLK), BF),
            pltpu.VMEM((2, 4, 4, 2, 32, BLK), BF),
            pltpu.VMEM((2, 2, 2, 32, D), BF),
            pltpu.VMEM((NY - 1, 32, BLK), BF),
            dma((7,)),
            dma((4,)),
            dma((2,)),
            dma((2, 3)),
            dma((2, 2)),
            dma((2, 4, 2)),
            dma((2, 4, 2)),
            dma((2, 4, NX)),
            dma((2, 4, NX)),
            dma((2, 2, NY, 2)),
            dma((2, 2, NY, 2)),
            dma((2, 4, 4)),
            dma((2, 4, 4)),
            dma((2, 2, 2)),
            dma((2, 2, 2)),
            dma((NY - 1,)),
            dma((NY - 1,)),
        ],
        compiler_params=pltpu.CompilerParams(
            collective_id=0, has_side_effects=True, vmem_limit_bytes=56 * 1024 * 1024
        ),
        cost_estimate=pl.CostEstimate(
            flops=12 * PAD * D * FF, bytes_accessed=10 * 1024 * 1024, transcendentals=2 * PAD * FF
        ),
    )(
        expert_ids.reshape(1, CAP),
        valid_counts,
        gate_values.reshape(1, CAP),
        tokens[0],
        cotangent[0],
        w_in[0],
        w_out.reshape(NY, BLK, D),
    )
    made = pl.pallas_call(
        place,
        out_shape=results,
        in_specs=[hbm] * 4,
        out_specs=(hbm,) * 4,
        scratch_shapes=[pltpu.VMEM(r.shape, r.dtype) for r in results] + [dma((2, 4))],
        compiler_params=pltpu.CompilerParams(vmem_limit_bytes=60 * 1024 * 1024),
    )(*made)
    return tuple(array[None] for array in made)


def solution(mesh):
    placed = (
        P("replica", "expert", None),
        P("replica", "expert", None),
        P("expert", None, None),
        P("expert", None, None),
        P("replica", "expert", None),
        P("replica", "expert", None),
        P("replica", "expert"),
    )
    return jax.shard_map(
        per_device,
        mesh=mesh,
        in_specs=placed,
        out_specs=(
            P("replica", "expert", None),
            P("replica", "expert", None),
            P("expert", "replica", None),
            P("expert", "replica", None),
        ),
        check_vma=False,
    )
```
